32 devices in a mesh: rep: 4 (over y, x), fsdp: 2 (over core), tp: 4 (over z).
Axes of the slice: x: 2, y: 2, z: 4, core: 2. Of those that a mesh axis runs over, the one named last changes fastest.
Arguments:
- tokens: bfloat16 [8192, 2048], P(('rep', 'fsdp'), 'tp'), may hold values from -6 to 6
- cotangent: bfloat16 [8192, 2048], P(('rep', 'fsdp'), 'tp'), may hold values from -6 to 6
- frame_mask: int32 [8192], P(('rep', 'fsdp')), may hold values 0 or 1
- ln_gain: bfloat16 [2048], P('tp'), may hold values from 0.099609375 to 1.8984375
- ln_bias: bfloat16 [2048], P('tp'), may hold values from -3 to 3
- weight_in: bfloat16 [2048, 8192], P('fsdp', 'tp'), may hold values from -0.1875 to 0.1875
- weight_out: bfloat16 [8192, 2048], P('tp', 'fsdp'), may hold values from -0.09375 to 0.09375
- blocks_in: int32 [16, 64], P('fsdp', 'tp'), may hold values 0 or 1
- blocks_out: int32 [64, 16], P('tp', 'fsdp'), may hold values 0 or 1
Outputs:
- block_out: bfloat16 [8192, 2048], P(('rep', 'fsdp'), 'tp')
- input_grad: bfloat16 [8192, 2048], P(('rep', 'fsdp'), 'tp')
- grad_in: float32 [2048, 8192], P('fsdp', 'tp')
- grad_out: float32 [8192, 2048], P('tp', 'fsdp')
- grad_gain: float32 [2048], P('tp')
- grad_bias: float32 [2048], P('tp')
The draws below stay inside these ranges and needn't reach their ends.
All inputs are finite; a program needn't handle non-finite values. No bound on the sum of `frame_mask` or of `blocks_in` or of `blocks_out` on one device may be relied on, other than what follows from the above.
Results may differ from the reference program's by a relative error of at most 0.019.
Values may be sent and summed in bfloat16 or wider, within the bound.
A program may use at most 128 MiB of HBM per device.

```python
from functools import partial
import jax
import jax.numpy as jnp
from jax import lax

D = 2048
FF = 8192
BLK = 128
TOK_DEV = 1024
TOKENS = 8192
N_REP = 4
N_FSDP = 2
N_TP = 4


def plant(result, own_key, smallest, high):
    longest = result.shape.index(max(result.shape))
    spots = []
    for shift in (0, 1):
        where = [jax.random.randint(jax.random.fold_in(own_key, axis), (), 0, length) for axis, length in enumerate(result.shape)]
        where[longest] = (where[longest] + shift) % result.shape[longest]
        spots.append(tuple(where))
    return result.at[spots[0]].set(smallest).at[spots[1]].set(high)


def level_of(rng, shape, cuts, smallest, largest):
    level = 1.0
    for dim, blocks in cuts:
        steps = jax.random.uniform(jax.random.fold_in(jax.random.fold_in(rng, 6), dim), (blocks,), jnp.float32, smallest / len(cuts), largest / len(cuts))
        level = level * jnp.repeat(jnp.exp(steps), shape[dim] // blocks).reshape((-1,) + (1,) * (len(shape) - 1 - dim))
    return level


def normal_values(key, extent, width, reach, cuts=(), kind=jnp.bfloat16):
    factor_of = level_of(key, extent, cuts, -0.22, 0.18) if cuts else 1.0
    result = jax.random.normal(key, extent, jnp.float32) * width * factor_of
    return jnp.minimum(jnp.maximum(result, -reach), reach).astype(kind)


def setup_inputs(seed: int = 0) -> dict:
    seeds = jax.random.split(jax.random.key(seed), 10)
    return {
        "tokens": normal_values(seeds[0], (TOKENS, D), 1.0, 6.0, ((0, 8), (1, 4))),
        "cotangent": normal_values(seeds[1], (TOKENS, D), 1.0, 6.0, ((0, 8), (1, 4))),
        "frame_mask": plant((jax.random.randint(seeds[2], (TOKENS,), 0, 2) < 1).astype(jnp.int32), jax.random.fold_in(seeds[2], 1), 0, 1),
        "ln_gain": jnp.clip(1.0 + 0.18 * jax.random.normal(seeds[3], (D,), jnp.float32), 0.099609375, 1.8984375).astype(jnp.bfloat16),
        "ln_bias": normal_values(seeds[4], (D,), 0.5, 3.0, ((0, 4),)),
        "weight_in": normal_values(seeds[5], (D, FF), (D // 2) ** -0.5, 0.1875, ((0, 2), (1, 4))),
        "weight_out": normal_values(seeds[6], (FF, D), (FF // 2) ** -0.5, 0.09375, ((0, 4), (1, 2))),
        "blocks_in": plant((jax.random.randint(seeds[7], (D // BLK, FF // BLK), 0, 2) < 1).astype(jnp.int32), jax.random.fold_in(seeds[7], 1), 0, 1),
        "blocks_out": plant((jax.random.randint(seeds[8], (FF // BLK, D // BLK), 0, 2) < 1).astype(jnp.int32), jax.random.fold_in(seeds[8], 1), 0, 1),
    }


def spread_blocks(blocks):
    return jnp.repeat(jnp.repeat(blocks, BLK, axis=0), BLK, axis=1)

def round_keep(array):
    return lax.optimization_barrier(array.astype(jnp.bfloat16)).astype(jnp.float32)

def reference(tokens, cotangent, frame_mask, ln_gain, ln_bias, weight_in, weight_out, blocks_in, blocks_out):
    groups = N_REP * N_FSDP
    local_cols = FF // N_TP
    masked_in = weight_in * spread_blocks(blocks_in).astype(jnp.bfloat16)
    masked_out = weight_out * spread_blocks(blocks_out).astype(jnp.bfloat16)
    gain_full = ln_gain.astype(jnp.float32)
    bias_full = ln_bias.astype(jnp.float32)
    gelu_exact = partial(jax.nn.gelu, approximate=False)
    split_in = masked_in.astype(jnp.float32).reshape(D, N_TP, local_cols)
    split_out = masked_out.astype(jnp.float32).reshape(N_TP, local_cols, D)

    def per_group(totals, inputs):
        sum_in, sum_out, sum_gain, sum_bias = totals
        token_rows, upstream, frame_flags = inputs
        values = token_rows.astype(jnp.float32)
        centre = lax.optimization_barrier(jnp.mean(values, axis=1, keepdims=True))
        centred = values - centre
        inv_std = lax.rsqrt(lax.optimization_barrier(jnp.mean(centred * centred, axis=1, keepdims=True)) + 1e-05)
        normed = centred * inv_std
        scaled = (normed * gain_full + bias_full).astype(jnp.bfloat16)
        hidden = jnp.dot(scaled, masked_in, preferred_element_type=jnp.float32)
        active = gelu_exact(hidden).astype(jnp.bfloat16)
        pieces = jnp.einsum('tkf,kfd->ktd', active.astype(jnp.float32).reshape(TOK_DEV, N_TP, local_cols), split_out)
        branch = lax.optimization_barrier(jnp.sum(round_keep(pieces), axis=0))
        output = (values + branch).astype(jnp.bfloat16)
        chosen = upstream * frame_flags[:, None].astype(jnp.bfloat16)
        back_active = jnp.dot(chosen, masked_out.T, preferred_element_type=jnp.float32)
        unused, gelu_back = jax.vjp(gelu_exact, hidden)
        back_hidden = gelu_back(back_active)[0].astype(jnp.bfloat16)
        pieces_in = jnp.einsum('tkf,dkf->ktd', back_hidden.astype(jnp.float32).reshape(TOK_DEV, N_TP, local_cols), split_in)
        back_normed = lax.optimization_barrier(jnp.sum(round_keep(pieces_in), axis=0))
        back_scaled = back_normed * gain_full
        mean_plain = lax.optimization_barrier(jnp.mean(back_scaled, axis=1, keepdims=True))
        mean_cross = lax.optimization_barrier(jnp.mean(back_scaled * normed, axis=1, keepdims=True))
        back_rows = inv_std * (back_scaled - mean_plain - normed * mean_cross)
        grad_rows = (chosen.astype(jnp.float32) + back_rows).astype(jnp.bfloat16)
        sum_gain = sum_gain + lax.optimization_barrier(jnp.sum(back_normed * normed, axis=0))
        sum_bias = sum_bias + lax.optimization_barrier(jnp.sum(back_normed, axis=0))
        term_in = jnp.dot(scaled.T, back_hidden, preferred_element_type=jnp.float32)
        term_out = jnp.dot(active.T, chosen, preferred_element_type=jnp.float32)
        sum_in = sum_in + round_keep(term_in)
        sum_out = sum_out + round_keep(term_out)
        return ((sum_in, sum_out, sum_gain, sum_bias), (output, grad_rows))
    start = (jnp.zeros((D, FF), jnp.float32), jnp.zeros((FF, D), jnp.float32), jnp.zeros((D,), jnp.float32), jnp.zeros((D,), jnp.float32))
    inputs = (tokens.reshape(groups, TOK_DEV, D), cotangent.reshape(groups, TOK_DEV, D), frame_mask.reshape(groups, TOK_DEV))
    totals, stacked = lax.scan(per_group, start, inputs)
    sum_in, sum_out, sum_gain, sum_bias = totals
    grad_in = sum_in * spread_blocks(blocks_in).astype(jnp.float32)
    grad_out = sum_out * spread_blocks(blocks_out).astype(jnp.float32)
    block_out = stacked[0].reshape(TOKENS, D)
    input_grad = stacked[1].reshape(TOKENS, D)
    return (block_out, input_grad, grad_in, grad_out, sum_gain, sum_bias)
```

```python
from functools import partial

import jax
import jax.numpy as jnp
from jax import lax
from jax.sharding import PartitionSpec as P

BLK = 128


def apply_blocks(weight, blocks, kind):
    row_blocks, col_blocks = blocks.shape
    shaped = weight.reshape(row_blocks, BLK, col_blocks, BLK)
    keeper = blocks.astype(kind)[:, None, :, None]
    return (shaped * keeper).reshape(weight.shape)


def contract_rows(left, right):
    return lax.dot_general(
        left, right, (((0,), (0,)), ((), ())), preferred_element_type=jnp.float32
    )


def contract_cols(left, right):
    return lax.dot_general(
        left, right, (((1,), (1,)), ((), ())), preferred_element_type=jnp.float32
    )


def flip(array, axis, size, bit):
    return lax.ppermute(array, axis, [(i, i ^ bit) for i in range(size)])


def cut(array, start, length, axis):
    return lax.dynamic_slice_in_dim(array, start, length, axis)


def put(array, piece, start, axis):
    return lax.dynamic_update_slice_in_dim(array, piece, start, axis)


def gather_pair(shard, axis):
    core = lax.axis_index("fsdp")
    width = shard.shape[axis]
    shape = list(shard.shape)
    shape[axis] = 2 * width
    other = flip(shard, "fsdp", 2, 1)
    whole = put(jnp.zeros(shape, shard.dtype), shard, core * width, axis)
    return put(whole, other, (1 - core) * width, axis)


def scatter_partials(partials, axis_name, size):
    me = lax.axis_index(axis_name)
    width = partials.shape[1] // size
    total = cut(partials, me * width, width, 1).astype(jnp.float32)
    for shift in range(1, size):
        target = lax.rem(me + shift, size)
        block = cut(partials, target * width, width, 1)
        got = lax.ppermute(
            block, axis_name, [(i, (i + shift) % size) for i in range(size)]
        )
        total = total + got.astype(jnp.float32)
    return total


def reduce_replicas(own, got, blocks, axis, n_rep):
    me = lax.axis_index("rep")
    total = own + got.astype(jnp.float32)
    half = total.shape[axis] // 2
    bits = [1 << k for k in range(n_rep.bit_length() - 1)]
    result = jnp.zeros(total.shape, jnp.float32)
    for part, order in ((0, bits), (1, bits[::-1])):
        held = lax.slice_in_dim(total, part * half, (part + 1) * half, axis=axis)
        start = part * half
        length = half
        trail = []
        for bit in order:
            length //= 2
            mine = jnp.where((me & bit) != 0, 1, 0)
            sent = cut(held, (1 - mine) * length, length, axis).astype(jnp.bfloat16)
            came = flip(sent, "rep", n_rep, bit)
            held = cut(held, mine * length, length, axis) + came.astype(jnp.float32)
            trail.append((bit, start + mine * length, start + (1 - mine) * length, length))
            start = start + mine * length
        held = held.astype(jnp.bfloat16)

        def place(result, piece, at, span):
            mask = cut(blocks, at // BLK, span // BLK, axis)
            return put(result, apply_blocks(piece.astype(jnp.float32), mask, jnp.float32), at, axis)

        result = place(result, held, start, length)
        for bit, own_at, other_at, length in trail[::-1]:
            came = flip(held, "rep", n_rep, bit)
            result = place(result, came, other_at, length)
            if bit != trail[0][0]:
                shape = list(held.shape)
                shape[axis] = 2 * length
                low = (me & bit) == 0
                held = jnp.where(
                    low,
                    jnp.concatenate([held, came], axis=axis),
                    jnp.concatenate([came, held], axis=axis),
                )
    return result


def on_device(
    n_rep,
    n_tp,
    tokens,
    cotangent,
    frame_mask,
    ln_gain,
    ln_bias,
    weight_in,
    weight_out,
    blocks_in,
    blocks_out,
):
    core = lax.axis_index("fsdp")
    whole_rows = lax.all_gather(tokens, "tp", axis=1, tiled=True)
    whole_grad = lax.all_gather(cotangent, "tp", axis=1, tiled=True)
    norm_full = lax.all_gather(jnp.stack([ln_gain, ln_bias]), "tp", axis=1, tiled=True)
    gain_full, bias_full = norm_full[0], norm_full[1]
    full_in = gather_pair(apply_blocks(weight_in, blocks_in, jnp.bfloat16), 0)
    full_out = gather_pair(apply_blocks(weight_out, blocks_out, jnp.bfloat16), 1)
    width = whole_rows.shape[1]
    half_width = width // 2
    own_width = tokens.shape[1]
    col_start = lax.axis_index("tp") * own_width
    gelu_exact = partial(jax.nn.gelu, approximate=False)
    values = whole_rows.astype(jnp.float32)
    centre = jnp.mean(values, axis=1, keepdims=True)
    centred = values - centre
    inv_std = lax.rsqrt(jnp.mean(centred * centred, axis=1, keepdims=True) + 1e-05)
    normed = centred * inv_std
    scaled = (normed * gain_full.astype(jnp.float32) + bias_full.astype(jnp.float32)).astype(
        jnp.bfloat16
    )
    scaled = lax.optimization_barrier(scaled)
    hidden = jnp.dot(scaled, full_in, preferred_element_type=jnp.float32)
    active = gelu_exact(hidden).astype(jnp.bfloat16)
    partial_out = jnp.dot(active, full_out, preferred_element_type=jnp.float32)
    branch = scatter_partials(partial_out.astype(jnp.bfloat16), "tp", n_tp)
    block_out = (tokens.astype(jnp.float32) + branch).astype(jnp.bfloat16)
    flags = frame_mask[:, None].astype(jnp.bfloat16)
    chosen = lax.optimization_barrier(whole_grad * flags)
    chosen_own = cotangent * flags

    own_at, other_at = core * half_width, (1 - core) * half_width
    out_other = contract_rows(active, cut(chosen, other_at, half_width, 1))
    out_got = flip(out_other.astype(jnp.bfloat16), "fsdp", 2, 1)
    out_own = contract_rows(active, cut(chosen, own_at, half_width, 1)).astype(jnp.bfloat16)
    grad_out = reduce_replicas(out_own.astype(jnp.float32), out_got, blocks_out, 1, n_rep)

    back_active = contract_cols(chosen, full_out)
    unused, gelu_back = jax.vjp(gelu_exact, hidden)
    back_hidden = gelu_back(back_active)[0].astype(jnp.bfloat16)

    in_other = contract_rows(cut(scaled, other_at, half_width, 1), back_hidden)
    in_got = flip(in_other.astype(jnp.bfloat16), "fsdp", 2, 1)
    in_own = contract_rows(cut(scaled, own_at, half_width, 1), back_hidden).astype(jnp.bfloat16)
    grad_in = reduce_replicas(in_own.astype(jnp.float32), in_got, blocks_in, 0, n_rep)

    partial_normed = contract_cols(back_hidden, full_in)
    normed_own = (
        tokens.astype(jnp.float32) - centre
    ) * inv_std
    gain_own = ln_gain.astype(jnp.float32)
    back_normed = lax.psum_scatter(
        partial_normed.astype(jnp.bfloat16), "tp", scatter_dimension=1, tiled=True
    ).astype(jnp.float32)
    back_scaled = back_normed * gain_own
    sum_plain = jnp.sum(back_scaled, axis=1)
    sum_cross = jnp.sum(back_scaled * normed_own, axis=1)
    sum_plain, sum_cross = lax.psum((sum_plain, sum_cross), "tp")
    mean_plain = (sum_plain / width)[:, None]
    mean_cross = (sum_cross / width)[:, None]
    back_rows = inv_std * (back_scaled - mean_plain - normed_own * mean_cross)
    input_grad = (chosen_own.astype(jnp.float32) + back_rows).astype(jnp.bfloat16)
    local_gain = jnp.sum(back_normed * normed_own, axis=0)
    local_bias = jnp.sum(back_normed, axis=0)
    grad_gain, grad_bias = lax.psum((local_gain, local_bias), ("rep", "fsdp"))
    return (block_out, input_grad, grad_in, grad_out, grad_gain, grad_bias)


def solution(mesh):
    placed = (
        P(("rep", "fsdp"), "tp"),
        P(("rep", "fsdp"), "tp"),
        P(("rep", "fsdp")),
        P("tp"),
        P("tp"),
        P("fsdp", "tp"),
        P("tp", "fsdp"),
        P("fsdp", "tp"),
        P("tp", "fsdp"),
    )
    return jax.shard_map(
        partial(on_device, mesh.shape["rep"], mesh.shape["tp"]),
        mesh=mesh,
        in_specs=placed,
        out_specs=(
            P(("rep", "fsdp"), "tp"),
            P(("rep", "fsdp"), "tp"),
            P("fsdp", "tp"),
            P("tp", "fsdp"),
            P("tp"),
            P("tp"),
        ),
        check_vma=False,
    )
```

```python
from functools import partial

import jax
import jax.numpy as jnp
from jax import lax
from jax.sharding import PartitionSpec as P

BLK = 128


def apply_blocks(weight, blocks, kind):
    row_blocks, col_blocks = blocks.shape
    shaped = weight.reshape(row_blocks, BLK, col_blocks, BLK)
    keeper = blocks.astype(kind)[:, None, :, None]
    return (shaped * keeper).reshape(weight.shape)


def contract_rows(left, right):
    return lax.dot_general(
        left, right, (((0,), (0,)), ((), ())), preferred_element_type=jnp.float32
    )


def contract_cols(left, right):
    return lax.dot_general(
        left, right, (((1,), (1,)), ((), ())), preferred_element_type=jnp.float32
    )


def flip(array, axis, size, bit):
    return lax.ppermute(array, axis, [(i, i ^ bit) for i in range(size)])


def cut(array, start, length, axis):
    return lax.dynamic_slice_in_dim(array, start, length, axis)


def put(array, piece, start, axis):
    return lax.dynamic_update_slice_in_dim(array, piece, start, axis)


def gather_pair(shard, axis):
    core = lax.axis_index("fsdp")
    width = shard.shape[axis]
    shape = list(shard.shape)
    shape[axis] = 2 * width
    other = flip(shard, "fsdp", 2, 1)
    whole = put(jnp.zeros(shape, shard.dtype), shard, core * width, axis)
    return put(whole, other, (1 - core) * width, axis)


def mask_rows(piece, blocks, start):
    span = piece.shape[0]
    wide = piece.astype(jnp.float32)
    if span % BLK == 0:
        return apply_blocks(wide, cut(blocks, start // BLK, span // BLK, 0), jnp.float32)
    keeper = cut(jnp.repeat(blocks.astype(jnp.float32), BLK, axis=0), start, span, 0)
    return wide * jnp.repeat(keeper, BLK, axis=1)


class ReplicaSum:
    def __init__(self, own, got, n_rep):
        self.own, self.got, self.n_rep = own, got, n_rep
        self.me = lax.axis_index("rep")
        self.bits = [1 << k for k in range(n_rep.bit_length() - 1)]
        half = own.shape[0] // 2
        self.lanes = []
        for part, order in ((0, self.bits), (1, self.bits[::-1])):
            self.lanes.append(
                {"order": order, "start": part * half, "length": half, "trail": []}
            )

    def halve(self, level):
        for lane in self.lanes:
            bit = lane["order"][level]
            lane["length"] //= 2
            length, base = lane["length"], lane["start"]
            mine = jnp.where((self.me & bit) != 0, 1, 0)
            keep_at, send_at = mine * length, (1 - mine) * length

            def fetch(at):
                if level:
                    return cut(lane["held"], at, length, 0)
                left = cut(self.own, base + at, length, 0).astype(jnp.float32)
                return left + cut(self.got, base + at, length, 0).astype(jnp.float32)

            lane["sent"] = fetch(send_at).astype(jnp.bfloat16)
            lane["kept"] = fetch(keep_at)
            lane["trail"].append((bit, base + send_at, length))
            lane["start"] = base + keep_at

    def take(self, name):
        return [lane[name] for lane in self.lanes]

    def give(self, name, values):
        for lane, value in zip(self.lanes, values):
            lane[name] = value

    def join(self, level):
        for lane in self.lanes:
            came = flip(lane["sent"], "rep", self.n_rep, lane["order"][level])
            lane["held"] = lane["kept"] + came.astype(jnp.float32)

    def spread(self, blocks, beside=None):
        result = jnp.zeros(self.own.shape, jnp.float32)
        for lane in self.lanes:
            lane["held"] = lane["held"].astype(jnp.bfloat16)
            result = put(result, mask_rows(lane["held"], blocks, lane["start"]), lane["start"], 0)
        for level in range(len(self.bits))[::-1]:
            for lane in self.lanes:
                bit, other_at, length = lane["trail"][level]
                held = lane["held"]
                came = flip(held, "rep", self.n_rep, bit)
                if beside is not None and level == 0:
                    came, beside = lax.optimization_barrier((came, beside))
                result = put(result, mask_rows(came, blocks, other_at), other_at, 0)
                if level:
                    lane["held"] = jnp.where(
                        (self.me & bit) == 0,
                        jnp.concatenate([held, came], axis=0),
                        jnp.concatenate([came, held], axis=0),
                    )
        return result, beside


def on_device(
    n_rep,
    tokens,
    cotangent,
    frame_mask,
    ln_gain,
    ln_bias,
    weight_in,
    weight_out,
    blocks_in,
    blocks_out,
):
    core = lax.axis_index("fsdp")
    whole_rows = lax.all_gather(tokens, "tp", axis=1, tiled=True)
    whole_grad = lax.all_gather(cotangent, "tp", axis=1, tiled=True)
    norm_full = lax.all_gather(jnp.stack([ln_gain, ln_bias]), "tp", axis=1, tiled=True)
    gain_full, bias_full = norm_full[0], norm_full[1]
    full_in = gather_pair(apply_blocks(weight_in, blocks_in, jnp.bfloat16), 0)
    full_out = gather_pair(apply_blocks(weight_out, blocks_out, jnp.bfloat16), 1)
    width = whole_rows.shape[1]
    half_width = width // 2
    own_width = tokens.shape[1]
    col_start = lax.axis_index("tp") * own_width
    gelu_exact = partial(jax.nn.gelu, approximate=False)
    values = whole_rows.astype(jnp.float32)
    centre = jnp.mean(values, axis=1, keepdims=True)
    centred = values - centre
    inv_std = lax.rsqrt(jnp.mean(centred * centred, axis=1, keepdims=True) + 1e-05)
    normed = centred * inv_std
    scaled = (normed * gain_full.astype(jnp.float32) + bias_full.astype(jnp.float32)).astype(
        jnp.bfloat16
    )
    scaled = lax.optimization_barrier(scaled)
    hidden = jnp.dot(scaled, full_in, preferred_element_type=jnp.float32)
    active = gelu_exact(hidden).astype(jnp.bfloat16)
    partial_out = jnp.dot(active, full_out, preferred_element_type=jnp.float32)
    partial_out = partial_out.astype(jnp.bfloat16)
    whole_grad, hidden, active, partial_out = lax.optimization_barrier(
        (whole_grad, hidden, active, partial_out)
    )
    branch = lax.psum_scatter(partial_out, "tp", scatter_dimension=1, tiled=True)
    flags = frame_mask[:, None].astype(jnp.bfloat16)
    chosen = lax.optimization_barrier(whole_grad * flags)
    chosen_own = cotangent * flags

    own_at, other_at = core * half_width, (1 - core) * half_width
    out_other = contract_rows(active, cut(chosen, other_at, half_width, 1)).astype(jnp.bfloat16)
    out_own = contract_rows(active, cut(chosen, own_at, half_width, 1)).astype(jnp.bfloat16)
    out_other, out_own, chosen = lax.optimization_barrier((out_other, out_own, chosen))
    out_got = flip(out_other, "fsdp", 2, 1)
    out_sum = ReplicaSum(out_own, out_got, n_rep)
    out_sum.halve(0)

    back_active = contract_cols(chosen, full_out)
    gelu_back = jax.vjp(gelu_exact, hidden)[1]
    back_hidden = gelu_back(back_active)[0].astype(jnp.bfloat16)

    back_hidden, sent = lax.optimization_barrier((back_hidden, out_sum.take("sent")))
    out_sum.give("sent", sent)
    out_sum.join(0)
    in_other = contract_rows(cut(scaled, other_at, half_width, 1), back_hidden)
    in_other = in_other.astype(jnp.bfloat16)
    in_own = contract_rows(cut(scaled, own_at, half_width, 1), back_hidden).astype(jnp.bfloat16)
    in_other, in_own, back_hidden = lax.optimization_barrier((in_other, in_own, back_hidden))
    in_got = flip(in_other, "fsdp", 2, 1)
    in_sum = ReplicaSum(in_own, in_got, n_rep)
    in_sum.halve(0)

    partial_normed = contract_cols(back_hidden, full_in).astype(jnp.bfloat16)
    back_normed = lax.psum_scatter(
        partial_normed, "tp", scatter_dimension=1, tiled=True
    ).astype(jnp.float32)
    branch, held, sent, partial_normed = lax.optimization_barrier(
        (branch, out_sum.take("held"), in_sum.take("sent"), partial_normed)
    )
    block_out = (tokens.astype(jnp.float32) + branch.astype(jnp.float32)).astype(jnp.bfloat16)
    out_sum.give("held", held)
    in_sum.give("sent", sent)
    in_sum.join(0)
    for level in range(1, len(out_sum.bits)):
        out_sum.halve(level)
        out_sum.join(level)
        in_sum.halve(level)
        in_sum.join(level)
    normed_own = (
        tokens.astype(jnp.float32) - centre
    ) * inv_std
    gain_own = ln_gain.astype(jnp.float32)
    back_scaled = back_normed * gain_own
    sum_plain = jnp.sum(back_scaled, axis=1)
    sum_cross = jnp.sum(back_scaled * normed_own, axis=1)
    sum_plain, sum_cross = lax.psum((sum_plain, sum_cross), "tp")
    local_gain = jnp.sum(back_normed * normed_own, axis=0)
    local_bias = jnp.sum(back_normed, axis=0)
    grad_gain, grad_bias = lax.psum((local_gain, local_bias), ("rep", "fsdp"))
    grad_out, unused = out_sum.spread(blocks_out)
    grad_in, (sum_plain, sum_cross, grad_gain, grad_bias) = in_sum.spread(
        blocks_in, (sum_plain, sum_cross, grad_gain, grad_bias)
    )
    mean_plain = (sum_plain / width)[:, None]
    mean_cross = (sum_cross / width)[:, None]
    back_rows = inv_std * (back_scaled - mean_plain - normed_own * mean_cross)
    input_grad = (chosen_own.astype(jnp.float32) + back_rows).astype(jnp.bfloat16)
    return (block_out, input_grad, grad_in, grad_out, grad_gain, grad_bias)


def solution(mesh):
    placed = (
        P(("rep", "fsdp"), "tp"),
        P(("rep", "fsdp"), "tp"),
        P(("rep", "fsdp")),
        P("tp"),
        P("tp"),
        P("fsdp", "tp"),
        P("tp", "fsdp"),
        P("fsdp", "tp"),
        P("tp", "fsdp"),
    )
    return jax.shard_map(
        partial(on_device, mesh.shape["rep"]),
        mesh=mesh,
        in_specs=placed,
        out_specs=(
            P(("rep", "fsdp"), "tp"),
            P(("rep", "fsdp"), "tp"),
            P("fsdp", "tp"),
            P("tp", "fsdp"),
            P("tp"),
            P("tp"),
        ),
        check_vma=False,
    )
```
